32 devices in a mesh: dp: 8 (over y, x, core), mp: 4 (over z).
Axes of the slice: x: 2, y: 2, z: 4, core: 2. Of those that a mesh axis runs over, the one named last changes fastest.
Arguments:
- response_query: bfloat16 [384, 8, 6144], P('dp', None, 'mp'), may hold values from -80 to 80, as said below
- response_keys: bfloat16 [2, 384, 8, 768], P(None, 'dp'), may hold values from -8 to 8
- prompt_cache: bfloat16 [2, 8, 1024, 768], P(None, 'dp'), may hold values from -6 to 6
- lengths: int32 [384], P('dp'), may hold values from 1 to 8, as said below
- owners: int32 [384], P('dp'), may hold values from 0 to 7, as said below
- pairing: int32 [384], replicated, may hold values from 0 to 383, each once
- residual: bfloat16 [384, 8192], P(None, 'dp'), may hold values from -90 to 90
- output_weight: bfloat16 [6144, 8192], P('mp', 'dp'), may hold values from -0.3125 to 0.3125
- norm_gain: float32 [8192], P('dp'), may hold values from 0.1 to 1.9
- reward_head: float32 [8192], P('dp'), may hold values from -0.0625 to 0.0625
Outputs:
- attention_rows: bfloat16 [384, 8, 6144], P('dp', None, 'mp')
- rewards: float32 [384], replicated
- pair_loss: float32 [], replicated
- weight_gradient: float32 [6144, 8192], P('mp', 'dp')
- head_gradient: float32 [8192], P('dp')
- pooled_gradient: float32 [384, 6144], P('dp', 'mp')
The draws below stay inside these ranges and needn't reach their ends.
Inputs may be any that keep to these rules, and one draw needn't show every extreme that they name: `response_query`: drawn jointly with response_keys. `lengths`: every dp index holds a response of length 8. The responses of one dp index spread over owners as evenly as possible: each owner receives at most 6 of them, and some owner receives exactly 6.
All inputs are finite; a program needn't handle non-finite values.
Results may differ from the reference program's by a relative error of at most 0.0056.
Values may be sent and summed in bfloat16 or wider, within the bound.
A program may use at most 64 MiB of HBM per device.

```python
import math
import jax
import jax.numpy as jnp
from jax import lax

D = 8192
HD = 128
Q_HEADS = 48
KV_HEADS = 6
SLOT = 8
RESP_DEV = 48
PREFIX = 1024
RESPONSES = 384
N_DP = 8


def query_and_keys(key):
    first, second = jax.random.split(jax.random.fold_in(key, 11), 2)
    queries = jnp.clip(jax.random.normal(first, (RESPONSES, SLOT, Q_HEADS, HD)), -6.0, 6.0)
    keys_values = jnp.clip(jax.random.normal(second, (2, RESPONSES, SLOT, KV_HEADS, HD)), -6.0, 6.0)
    return (queries.reshape(RESPONSES, SLOT, Q_HEADS * HD), keys_values.reshape(2, RESPONSES, SLOT, KV_HEADS * HD))


def draw_response_query(key, part):
    return query_and_keys(key)[0].astype(jnp.bfloat16)


def draw_response_keys(key, part):
    return query_and_keys(key)[1].astype(jnp.bfloat16)


def draw_lengths(key, part):
    devices = RESPONSES // RESP_DEV
    base = jax.random.randint(key, (devices, RESP_DEV), 1, SLOT + 1)
    longest = jax.random.randint(jax.random.fold_in(key, 7), (devices,), 0, RESP_DEV)
    hits = jnp.arange(RESP_DEV)[None, :] == longest[:, None]
    return jnp.where(hits, SLOT, base).reshape(RESPONSES).astype(jnp.int32)


def draw_owners(key, part):
    devices = RESPONSES // RESP_DEV
    device_keys = jax.random.split(jax.random.fold_in(key, 5), devices)
    orders = jax.vmap(lambda single: jax.random.permutation(single, devices))(device_keys)
    columns = jnp.arange(RESP_DEV) % devices
    return orders[:, columns].reshape(RESPONSES).astype(jnp.int32)


def draw_residual(key, part):
    first, second, third = jax.random.split(jax.random.fold_in(key, 3), 3)
    row_scale = jnp.exp(jax.random.uniform(first, (RESPONSES, 1), minval=math.log(0.5), maxval=math.log(5.0)))
    column_scale = jnp.exp(jax.random.uniform(second, (1, D), minval=math.log(0.3), maxval=math.log(3.0)))
    base = jnp.clip(jax.random.normal(third, (RESPONSES, D)), -6.0, 6.0)
    return (base * row_scale * column_scale).astype(jnp.bfloat16)


def steps_of(stream_key, dims, shards, low, high):
    level, own = 1.0, jax.random.fold_in(stream_key, 6)
    for axis_at, blocks in shards:
        heights = jnp.exp(jax.random.uniform(jax.random.fold_in(own, axis_at), (blocks,), jnp.float32, low / len(shards), high / len(shards)))
        level = level * jnp.repeat(heights, dims[axis_at] // blocks).reshape([-1 if axis == axis_at else 1 for axis in range(len(dims))])
    return level


def scatter_about(own_key, shape, scale, most, shards=(), dtype=jnp.bfloat16):
    values = scale * jax.random.normal(own_key, shape, jnp.float32)
    if shards:
        values = values * steps_of(own_key, shape, shards, -0.22, 0.18)
    return jnp.clip(values, -most, most).astype(dtype)


def setup_inputs(seed: int = 0) -> dict:
    keys = jax.random.split(jax.random.key(seed), 11)
    response_query = draw_response_query(jax.random.fold_in(keys[10], 71), 0)
    response_keys = draw_response_keys(jax.random.fold_in(keys[10], 71), 0)
    prompt_cache = scatter_about(keys[2], (2, N_DP, PREFIX, KV_HEADS * HD), 1.0, 6.0, ((1, 8),))
    lengths = draw_lengths(jax.random.fold_in(keys[10], 71), 0)
    owners = draw_owners(jax.random.fold_in(keys[10], 71), 0)
    pairing = jax.random.permutation(keys[5], RESPONSES).astype(jnp.int32)
    residual = draw_residual(jax.random.fold_in(keys[10], 71), 0)
    output_weight = scatter_about(keys[7], (Q_HEADS * HD, D), (Q_HEADS * HD // 16) ** -0.5, 0.3125, ((0, 4), (1, 8)))
    norm_gain = jnp.clip(1.0 + 0.18 * jax.random.normal(keys[8], (D,), jnp.float32), 0.1, 1.9)
    reward_head = scatter_about(keys[9], (D,), D ** -0.5, 0.0625, ((0, 8),), jnp.float32)
    return {"response_query": response_query, "response_keys": response_keys, "prompt_cache": prompt_cache, "lengths": lengths, "owners": owners, "pairing": pairing, "residual": residual, "output_weight": output_weight, "norm_gain": norm_gain, "reward_head": reward_head}


EPSILON = 1e-05

def bradley_terry(rewards, pairing):
    chosen = pairing[0::2]
    rejected = pairing[1::2]
    margin = rewards[chosen] - rewards[rejected]
    loss_value = jnp.mean(jax.nn.softplus(-margin))
    slope = -jax.nn.sigmoid(-margin) / margin.shape[0]
    reward_slope = jnp.zeros_like(rewards).at[chosen].add(slope).at[rejected].add(-slope)
    return (loss_value, reward_slope)

def round_weights(values):
    return lax.optimization_barrier(values.astype(jnp.bfloat16)).astype(jnp.float32)

def reference(response_query, response_keys, prompt_cache, lengths, owners, pairing, residual, output_weight, norm_gain, reward_head):
    score_scale = 1.0 / math.sqrt(HD)
    group_size = Q_HEADS // KV_HEADS
    offsets = jnp.arange(SLOT)

    def attend(item):
        query_rows, key_rows, length, owner_index = item
        prompt = lax.dynamic_index_in_dim(prompt_cache, owner_index, axis=1, keepdims=False)
        queries = query_rows.reshape(SLOT, KV_HEADS, group_size, HD).astype(jnp.float32)
        cache_keys = prompt[0].reshape(PREFIX, KV_HEADS, HD).astype(jnp.float32)
        cache_values = prompt[1].reshape(PREFIX, KV_HEADS, HD).astype(jnp.float32)
        own_keys = key_rows[0].reshape(SLOT, KV_HEADS, HD).astype(jnp.float32)
        own_values = key_rows[1].reshape(SLOT, KV_HEADS, HD).astype(jnp.float32)
        far_scores = jnp.einsum('tkgh,pkh->kgtp', queries, cache_keys) * score_scale
        near_scores = jnp.einsum('tkgh,skh->kgts', queries, own_keys) * score_scale
        allowed = (offsets[None, :] <= offsets[:, None]) & (offsets[None, :] < length)
        near_scores = jnp.where(allowed[None, None], near_scores, -jnp.inf)
        row_top = jnp.maximum(lax.optimization_barrier(jnp.max(far_scores, axis=-1)), lax.optimization_barrier(jnp.max(near_scores, axis=-1)))
        far_weight = jnp.exp(far_scores - row_top[..., None])
        near_weight = jnp.exp(near_scores - row_top[..., None])
        weight_total = lax.optimization_barrier(jnp.sum(far_weight, axis=-1)) + lax.optimization_barrier(jnp.sum(near_weight, axis=-1))
        output = jnp.einsum('kgtp,pkh->tkgh', round_weights(far_weight), cache_values)
        output = output + jnp.einsum('kgts,skh->tkgh', round_weights(near_weight), own_values)
        output = output / jnp.transpose(weight_total, (2, 0, 1))[..., None]
        output = jnp.where((offsets < length)[:, None, None, None], output, 0.0)
        return output.reshape(SLOT, Q_HEADS * HD).astype(jnp.bfloat16)
    attention_rows = lax.map(attend, (response_query, jnp.moveaxis(response_keys, 1, 0), lengths, owners))
    pooled = attention_rows[jnp.arange(RESPONSES), lengths - 1]
    combined = jnp.dot(pooled, output_weight, preferred_element_type=jnp.float32) + residual.astype(jnp.float32)
    scaled_head = norm_gain * reward_head
    square_sum = lax.optimization_barrier(jnp.sum(combined * combined, axis=1))
    signal = lax.optimization_barrier(jnp.sum(combined * scaled_head[None, :], axis=1))
    inverse = lax.rsqrt(square_sum / D + EPSILON)
    rewards = inverse * signal
    pair_loss, reward_slope = bradley_terry(rewards, pairing)
    direct_term = reward_slope * inverse
    norm_term = reward_slope * inverse * inverse * inverse * signal / D
    upstream = direct_term[:, None] * scaled_head[None, :] - norm_term[:, None] * combined
    upstream_half = upstream.astype(jnp.bfloat16)
    head_gradient = lax.optimization_barrier(jnp.sum(direct_term[:, None] * combined * norm_gain[None, :], axis=0))
    weight_gradient = jnp.dot(pooled.T, upstream_half, preferred_element_type=jnp.float32)
    pooled_gradient = jnp.dot(upstream_half, output_weight.T, preferred_element_type=jnp.float32)
    return (attention_rows, rewards, pair_loss, weight_gradient, head_gradient, pooled_gradient)
```

```python
import functools
import math

import jax
import jax.numpy as jnp
from jax import lax
from jax.experimental import pallas as pl
from jax.experimental.pallas import tpu as pltpu
from jax.sharding import PartitionSpec as P

D = 8192
HD = 128
Q_HEADS = 48
KV_HEADS = 6


EPSILON = 1e-05


def bradley_terry(rewards, pairing):
    count = rewards.shape[0]
    chosen = pairing[0::2, None] == jnp.arange(count)[None, :]
    rejected = pairing[1::2, None] == jnp.arange(count)[None, :]
    sign = chosen.astype(jnp.float32) - rejected.astype(jnp.float32)
    margin = jnp.sum(sign * rewards[None, :], axis=1)
    loss_value = jnp.mean(jax.nn.softplus(-margin))
    slope = -jax.nn.sigmoid(-margin) / margin.shape[0]
    reward_slope = jnp.sum(sign * slope[:, None], axis=0)
    return (loss_value, reward_slope)


def pack_kernel(window, meta, query, keys, out):
    slots = out.shape[0]
    width = query.shape[2]
    span = window * HD
    first = pl.multiple_of(meta[2 * slots] * HD, HD)

    def body(p, carry):
        r = meta[p]
        out[p, :, pl.ds(0, width)] = query[r]
        out[p, :, pl.ds(width, span)] = keys[0, r, :, pl.ds(first, span)]
        out[p, :, pl.ds(width + span, span)] = keys[1, r, :, pl.ds(first, span)]
        length = meta[slots + p].astype(jnp.float32)
        out[p, :, pl.ds(width + 2 * span, HD)] = jnp.full(
            (out.shape[1], HD), length, jnp.float32
        ).astype(jnp.bfloat16)
        return carry

    lax.fori_loop(0, slots, body, 0)


def attention_kernel(slot_count, meta, query, own_k, own_v, lens, cache, out):
    rows = query.shape[0]
    chunk = 128
    scale = math.log2(math.e) / math.sqrt(HD)
    contract = (((1,), (1,)), ((), ()))
    row = lax.broadcasted_iota(jnp.int32, (chunk, chunk), 0)
    col = lax.broadcasted_iota(jnp.int32, (chunk, chunk), 1)
    t = row % slot_count
    s = col % slot_count
    causal = (row // slot_count == col // slot_count) & (s <= t)
    s_float = s.astype(jnp.float32)
    t_float = t.astype(jnp.float32)
    for start in range(0, rows, chunk):
        here = pl.ds(start, chunk)
        q = query[here, :]
        length = lens[here, :].astype(jnp.float32)
        far = lax.dot_general(q, cache[0, 0], contract, preferred_element_type=jnp.float32)
        near = lax.dot_general(q, own_k[here, :], contract, preferred_element_type=jnp.float32)
        near = jnp.where(causal & (s_float < length), near, -jnp.inf)
        top = jnp.maximum(
            jnp.max(far, axis=1, keepdims=True), jnp.max(near, axis=1, keepdims=True)
        )
        far = jnp.exp2((far - top) * scale)
        near = jnp.exp2((near - top) * scale)
        total = jnp.sum(far, axis=1, keepdims=True) + jnp.sum(near, axis=1, keepdims=True)
        value = jnp.dot(far.astype(jnp.bfloat16), cache[1, 0], preferred_element_type=jnp.float32)
        value += jnp.dot(
            near.astype(jnp.bfloat16), own_v[here, :], preferred_element_type=jnp.float32
        )
        value = jnp.where(t_float < length, value / total, 0.0)
        out[here, :] = value.astype(jnp.bfloat16)


def unpack_kernel(meta, returned, out, pooled, last):
    held, slot_count, width = out.shape
    row = lax.broadcasted_iota(jnp.int32, (slot_count, width), 0)

    def body(r, carry):
        block = returned[meta[r]]
        out[r] = block
        picked = jnp.where(row == meta[held + r] - 1, block.astype(jnp.float32), 0.0)
        last[pl.ds(r, 1), :] = jnp.sum(picked, axis=0, keepdims=True)
        return carry

    lax.fori_loop(0, held, body, 0)
    pooled[...] = last[...].astype(jnp.bfloat16)


def shards(
    response_query,
    response_keys,
    prompt_cache,
    lengths,
    owners,
    pairing,
    residual,
    output_weight,
    norm_gain,
    reward_head,
):
    groups = lax.axis_size("dp")
    planes = lax.axis_size("mp")
    model_rank = lax.axis_index("mp")
    held_count, slot_count, head_width = response_query.shape
    local_heads = head_width // HD
    group_size = Q_HEADS // KV_HEADS
    per_owner = (held_count + groups - 1) // groups
    capacity = groups * per_owner
    window = max(
        (m * local_heads + local_heads - 1) // group_size - m * local_heads // group_size + 1
        for m in range(planes)
    )
    first_head = jnp.minimum(model_rank * local_heads // group_size, KV_HEADS - window)
    head_kv = (model_rank * local_heads + jnp.arange(local_heads)) // group_size
    positions = jnp.arange(held_count)
    earlier = (owners[None, :] == owners[:, None]) & (positions[None, :] < positions[:, None])
    target = (owners * per_owner + jnp.sum(earlier, axis=1)).astype(jnp.int32)
    sent_from = (target[None, :] == jnp.arange(capacity)[:, None]).astype(jnp.int32)
    source = jnp.sum(sent_from * positions[None, :], axis=1)
    slot_length = jnp.sum(sent_from * lengths[None, :], axis=1)
    params = pltpu.CompilerParams(vmem_limit_bytes=40 * 1024 * 1024)
    vmem = pl.BlockSpec(memory_space=pltpu.VMEM)
    smem = pl.BlockSpec(memory_space=pltpu.SMEM)
    packed_width = head_width + (2 * window + 1) * HD
    packed = pl.pallas_call(
        functools.partial(pack_kernel, window),
        out_shape=jax.ShapeDtypeStruct((capacity, slot_count, packed_width), jnp.bfloat16),
        in_specs=[smem, vmem, vmem],
        out_specs=vmem,
        compiler_params=params,
        name="pack",
    )(
        jnp.concatenate([source, slot_length, first_head[None]]).astype(jnp.int32),
        response_query,
        response_keys,
    )
    packed = packed.reshape(groups, per_owner, slot_count, packed_width)
    arrived = lax.all_to_all(packed, "dp", split_axis=0, concat_axis=0, tiled=True)
    rows = capacity * slot_count
    arrived = arrived.reshape(rows, packed_width)
    block = (rows, HD)
    attended = pl.pallas_call(
        functools.partial(attention_kernel, slot_count),
        out_shape=jax.ShapeDtypeStruct((rows, head_width), jnp.bfloat16),
        grid_spec=pltpu.PrefetchScalarGridSpec(
            num_scalar_prefetch=1,
            grid=(local_heads,),
            in_specs=[
                pl.BlockSpec(block, lambda h, meta: (0, h)),
                pl.BlockSpec(block, lambda h, meta: (0, local_heads + meta[local_heads + h])),
                pl.BlockSpec(
                    block, lambda h, meta: (0, local_heads + window + meta[local_heads + h])
                ),
                pl.BlockSpec(block, lambda h, meta: (0, local_heads + 2 * window)),
                pl.BlockSpec(
                    (2, 1, prompt_cache.shape[2], HD), lambda h, meta: (0, 0, 0, meta[h])
                ),
            ],
            out_specs=pl.BlockSpec(block, lambda h, meta: (0, h)),
        ),
        compiler_params=params,
        name="attention",
    )(
        jnp.concatenate([head_kv, head_kv - first_head]).astype(jnp.int32),
        arrived,
        arrived,
        arrived,
        arrived,
        prompt_cache,
    )
    result = attended.reshape(groups, per_owner, slot_count, head_width)
    returned = lax.all_to_all(result, "dp", split_axis=0, concat_axis=0, tiled=True)
    attention_rows, pooled_local = pl.pallas_call(
        unpack_kernel,
        out_shape=(
            jax.ShapeDtypeStruct(response_query.shape, jnp.bfloat16),
            jax.ShapeDtypeStruct((held_count, head_width), jnp.bfloat16),
        ),
        in_specs=[smem, vmem],
        out_specs=(vmem, vmem),
        scratch_shapes=[pltpu.VMEM((held_count, head_width), jnp.float32)],
        compiler_params=params,
        name="unpack",
    )(
        jnp.concatenate([target, lengths]).astype(jnp.int32),
        returned.reshape(capacity, slot_count, head_width),
    )
    pooled_all = lax.all_gather(pooled_local, "dp", axis=0, tiled=True)
    count = pooled_all.shape[0]
    share = count // planes
    partial_mix = jnp.dot(pooled_all, output_weight, preferred_element_type=jnp.float32)
    columns = output_weight.shape[1]
    scaled_head = norm_gain * reward_head
    shares = lax.all_to_all(
        partial_mix.astype(jnp.bfloat16).reshape(planes, share, columns),
        "mp",
        split_axis=0,
        concat_axis=0,
        tiled=True,
    )
    part = jnp.sum(shares.astype(jnp.float32), axis=0) + lax.dynamic_slice_in_dim(
        residual, model_rank * share, share, 0
    ).astype(jnp.float32)
    combined = lax.all_gather(part.astype(jnp.bfloat16), "mp", axis=0, tiled=True).astype(
        jnp.float32
    )
    sums = jnp.stack([jnp.sum(part * part, axis=1), jnp.sum(part * scaled_head[None, :], axis=1)])
    sums = lax.dynamic_update_slice(
        jnp.zeros((2, count), jnp.float32), sums, (jnp.int32(0), model_rank * share)
    )
    square_sum, signal = lax.psum(sums, ("dp", "mp"))
    inverse = lax.rsqrt(square_sum / D + EPSILON)
    rewards = inverse * signal
    pair_loss, reward_slope = bradley_terry(rewards, pairing)
    direct_term = reward_slope * inverse
    norm_term = reward_slope * inverse * inverse * inverse * signal / D
    upstream = direct_term[:, None] * scaled_head[None, :] - norm_term[:, None] * combined
    head_gradient = jnp.sum(direct_term[:, None] * combined * norm_gain[None, :], axis=0)
    upstream_half = upstream.astype(jnp.bfloat16)
    slope_part = lax.dot_general(
        upstream_half,
        output_weight,
        (((1,), (1,)), ((), ())),
        preferred_element_type=jnp.float32,
    ).astype(jnp.bfloat16)
    slope_parts = lax.all_to_all(
        slope_part.reshape(groups, held_count, head_width),
        "dp",
        split_axis=0,
        concat_axis=0,
        tiled=True,
    )
    weight_gradient = lax.dot_general(
        pooled_all, upstream_half, (((0,), (0,)), ((), ())), preferred_element_type=jnp.float32
    )
    pooled_gradient = jnp.sum(slope_parts.astype(jnp.float32), axis=0)
    return (attention_rows, rewards, pair_loss, weight_gradient, head_gradient, pooled_gradient)


def solution(mesh):
    placed = (
        P("dp", None, "mp"),
        P(None, "dp", None, None),
        P(None, "dp", None, None),
        P("dp"),
        P("dp"),
        P(),
        P(None, "dp"),
        P("mp", "dp"),
        P("dp"),
        P("dp"),
    )
    return jax.shard_map(
        shards,
        mesh=mesh,
        in_specs=placed,
        out_specs=(P("dp", None, "mp"), P(), P(), P("mp", "dp"), P("dp"), P("dp", "mp")),
        check_vma=False,
    )
```

```python
import functools
import math

import jax
import jax.numpy as jnp
from jax import lax
from jax.experimental import pallas as pl
from jax.experimental.pallas import tpu as pltpu
from jax.sharding import PartitionSpec as P

D = 8192
HD = 128
Q_HEADS = 48
KV_HEADS = 6


EPSILON = 1e-05


def bradley_terry(rewards, pairing):
    count = rewards.shape[0]
    chosen = pairing[0::2, None] == jnp.arange(count)[None, :]
    rejected = pairing[1::2, None] == jnp.arange(count)[None, :]
    sign = chosen.astype(jnp.float32) - rejected.astype(jnp.float32)
    margin = jnp.sum(sign * rewards[None, :], axis=1)
    loss_value = jnp.mean(jax.nn.softplus(-margin))
    slope = -jax.nn.sigmoid(-margin) / margin.shape[0]
    reward_slope = jnp.sum(sign * slope[:, None], axis=0)
    return (loss_value, reward_slope)


def pack_kernel(window, meta, query, keys, out):
    slots = out.shape[0]
    width = query.shape[2]
    span = window * HD
    first = pl.multiple_of(meta[2 * slots] * HD, HD)

    def body(p, carry):
        r = meta[p]
        out[p, :, pl.ds(0, width)] = query[r]
        out[p, :, pl.ds(width, span)] = keys[0, r, :, pl.ds(first, span)]
        out[p, :, pl.ds(width + span, span)] = keys[1, r, :, pl.ds(first, span)]
        length = meta[slots + p].astype(jnp.float32)
        place = r.astype(jnp.float32)
        lane = lax.broadcasted_iota(jnp.int32, (out.shape[1], HD), 1)
        out[p, :, pl.ds(width + 2 * span, HD)] = jnp.where(lane < HD // 2, length, place).astype(
            jnp.bfloat16
        )
        return carry

    lax.fori_loop(0, slots, body, 0)


def attention_kernel(slot_count, meta, query, own_k, own_v, lens, cache, out, pooled):
    rows = query.shape[0]
    head = pl.program_id(0)
    chunk = 128
    blocks = chunk // slot_count
    scale = math.log2(math.e) / math.sqrt(HD)
    contract = (((1,), (1,)), ((), ()))
    row = lax.broadcasted_iota(jnp.int32, (chunk, chunk), 0)
    col = lax.broadcasted_iota(jnp.int32, (chunk, chunk), 1)
    t = row % slot_count
    s = col % slot_count
    causal = (row // slot_count == col // slot_count) & (s <= t)
    s_float = s.astype(jnp.float32)
    t_float = t.astype(jnp.float32)
    for start in range(0, rows, chunk):
        here = pl.ds(start, chunk)
        q = query[here, :]
        length = jnp.broadcast_to(lens[here, :].astype(jnp.float32)[:, 0:1], (chunk, chunk))
        far = lax.dot_general(q, cache[0, 0], contract, preferred_element_type=jnp.float32)
        near = lax.dot_general(q, own_k[here, :], contract, preferred_element_type=jnp.float32)
        near = jnp.where(causal & (s_float < length), near, -jnp.inf)
        top = jnp.maximum(
            jnp.max(far, axis=1, keepdims=True), jnp.max(near, axis=1, keepdims=True)
        )
        far = jnp.exp2((far - top) * scale)
        near = jnp.exp2((near - top) * scale)
        total = jnp.sum(far, axis=1, keepdims=True) + jnp.sum(near, axis=1, keepdims=True)
        value = jnp.dot(far.astype(jnp.bfloat16), cache[1, 0], preferred_element_type=jnp.float32)
        value += jnp.dot(
            near.astype(jnp.bfloat16), own_v[here, :], preferred_element_type=jnp.float32
        )
        value = jnp.where(t_float < length, value / total, 0.0)
        out[here, :] = value.astype(jnp.bfloat16)
        last = jnp.where(t_float == length - 1.0, value, 0.0)
        last = jnp.sum(last.reshape(blocks, slot_count, HD), axis=1)
        there = pl.ds(start // slot_count, blocks)
        pooled[there, pl.ds(pl.multiple_of(head * HD, HD), HD)] = last.astype(jnp.bfloat16)

        @pl.when(head == 0)
        def _():
            place = lens[here, :].astype(jnp.float32).reshape(blocks, slot_count, HD)
            pooled[there, pl.ds(pooled.shape[1] - HD, HD)] = jnp.max(place, axis=1).astype(
                jnp.bfloat16
            )


def unpack_kernel(meta, returned, out):
    def body(r, carry):
        out[r] = returned[meta[r]]
        return carry

    lax.fori_loop(0, out.shape[0], body, 0)


def shards(
    response_query,
    response_keys,
    prompt_cache,
    lengths,
    owners,
    pairing,
    residual,
    output_weight,
    norm_gain,
    reward_head,
):
    groups = lax.axis_size("dp")
    planes = lax.axis_size("mp")
    model_rank = lax.axis_index("mp")
    held_count, slot_count, head_width = response_query.shape
    local_heads = head_width // HD
    group_size = Q_HEADS // KV_HEADS
    per_owner = (held_count + groups - 1) // groups
    capacity = groups * per_owner
    window = max(
        (m * local_heads + local_heads - 1) // group_size - m * local_heads // group_size + 1
        for m in range(planes)
    )
    first_head = jnp.minimum(model_rank * local_heads // group_size, KV_HEADS - window)
    head_kv = (model_rank * local_heads + jnp.arange(local_heads)) // group_size
    positions = jnp.arange(held_count)
    earlier = (owners[None, :] == owners[:, None]) & (positions[None, :] < positions[:, None])
    target = (owners * per_owner + jnp.sum(earlier, axis=1)).astype(jnp.int32)
    sent_from = (target[None, :] == jnp.arange(capacity)[:, None]).astype(jnp.int32)
    source = jnp.sum(sent_from * positions[None, :], axis=1)
    slot_length = jnp.sum(sent_from * lengths[None, :], axis=1)
    params = pltpu.CompilerParams(vmem_limit_bytes=40 * 1024 * 1024)
    vmem = pl.BlockSpec(memory_space=pltpu.VMEM)
    smem = pl.BlockSpec(memory_space=pltpu.SMEM)
    packed_width = head_width + (2 * window + 1) * HD
    packed = pl.pallas_call(
        functools.partial(pack_kernel, window),
        out_shape=jax.ShapeDtypeStruct((capacity, slot_count, packed_width), jnp.bfloat16),
        in_specs=[smem, vmem, vmem],
        out_specs=vmem,
        compiler_params=params,
        name="pack",
    )(
        jnp.concatenate([source, slot_length, first_head[None]]).astype(jnp.int32),
        response_query,
        response_keys,
    )
    packed = packed.reshape(groups, per_owner, slot_count, packed_width)
    arrived = lax.all_to_all(packed, "dp", split_axis=0, concat_axis=0, tiled=True)
    rows = capacity * slot_count
    arrived = arrived.reshape(rows, packed_width)
    block = (rows, HD)
    attended, pooled_sent = pl.pallas_call(
        functools.partial(attention_kernel, slot_count),
        out_shape=(
            jax.ShapeDtypeStruct((rows, head_width), jnp.bfloat16),
            jax.ShapeDtypeStruct((capacity, head_width + HD), jnp.bfloat16),
        ),
        grid_spec=pltpu.PrefetchScalarGridSpec(
            num_scalar_prefetch=1,
            grid=(local_heads,),
            in_specs=[
                pl.BlockSpec(block, lambda h, meta: (0, h)),
                pl.BlockSpec(block, lambda h, meta: (0, local_heads + meta[local_heads + h])),
                pl.BlockSpec(
                    block, lambda h, meta: (0, local_heads + window + meta[local_heads + h])
                ),
                pl.BlockSpec(block, lambda h, meta: (0, local_heads + 2 * window)),
                pl.BlockSpec(
                    (2, 1, prompt_cache.shape[2], HD), lambda h, meta: (0, 0, 0, meta[h])
                ),
            ],
            out_specs=(
                pl.BlockSpec(block, lambda h, meta: (0, h)),
                pl.BlockSpec((capacity, head_width + HD), lambda h, meta: (0, 0)),
            ),
        ),
        compiler_params=params,
        name="attention",
    )(
        jnp.concatenate([head_kv, head_kv - first_head]).astype(jnp.int32),
        arrived,
        arrived,
        arrived,
        arrived,
        prompt_cache,
    )
    pooled_slots = lax.all_gather(pooled_sent, "dp", axis=0, tiled=True)
    result = attended.reshape(groups, per_owner, slot_count, head_width)
    returned = lax.all_to_all(result, "dp", split_axis=0, concat_axis=0, tiled=True)
    attention_rows = pl.pallas_call(
        unpack_kernel,
        out_shape=jax.ShapeDtypeStruct(response_query.shape, jnp.bfloat16),
        in_specs=[smem, vmem],
        out_specs=vmem,
        compiler_params=params,
        name="unpack",
    )(target, returned.reshape(capacity, slot_count, head_width))
    count = held_count * groups
    sender = jnp.arange(capacity * groups) % capacity // per_owner
    place = pooled_slots[:, head_width + HD - 1].astype(jnp.int32)
    live = pooled_slots[:, head_width] > 0
    response = jnp.where(live, sender * held_count + place, count)
    order = (jnp.arange(count)[:, None] == response[None, :]).astype(jnp.bfloat16)
    pooled_all = jnp.dot(
        order, pooled_slots[:, :head_width], preferred_element_type=jnp.float32
    ).astype(jnp.bfloat16)
    share = count // planes
    partial_mix = jnp.dot(pooled_all, output_weight, preferred_element_type=jnp.float32)
    columns = output_weight.shape[1]
    scaled_head = norm_gain * reward_head
    shares = lax.all_to_all(
        partial_mix.astype(jnp.bfloat16).reshape(planes, share, columns),
        "mp",
        split_axis=0,
        concat_axis=0,
        tiled=True,
    )
    part = jnp.sum(shares.astype(jnp.float32), axis=0) + lax.dynamic_slice_in_dim(
        residual, model_rank * share, share, 0
    ).astype(jnp.float32)
    combined = lax.all_gather(part.astype(jnp.bfloat16), "mp", axis=0, tiled=True).astype(
        jnp.float32
    )
    square_sum = jnp.sum(combined * combined, axis=1)
    signal = jnp.sum(combined * scaled_head[None, :], axis=1)
    square_sum, signal = lax.psum((square_sum, signal), "dp")
    inverse = lax.rsqrt(square_sum / D + EPSILON)
    rewards = inverse * signal
    pair_loss, reward_slope = bradley_terry(rewards, pairing)
    direct_term = reward_slope * inverse
    norm_term = reward_slope * inverse * inverse * inverse * signal / D
    upstream = direct_term[:, None] * scaled_head[None, :] - norm_term[:, None] * combined
    head_gradient = jnp.sum(direct_term[:, None] * combined * norm_gain[None, :], axis=0)
    upstream_half = upstream.astype(jnp.bfloat16)
    slope_part = lax.dot_general(
        upstream_half,
        output_weight,
        (((1,), (1,)), ((), ())),
        preferred_element_type=jnp.float32,
    ).astype(jnp.bfloat16)
    slope_parts = lax.all_to_all(
        slope_part.reshape(groups, held_count, head_width),
        "dp",
        split_axis=0,
        concat_axis=0,
        tiled=True,
    )
    weight_gradient = lax.dot_general(
        pooled_all, upstream_half, (((0,), (0,)), ((), ())), preferred_element_type=jnp.float32
    )
    pooled_gradient = jnp.sum(slope_parts.astype(jnp.float32), axis=0)
    return (attention_rows, rewards, pair_loss, weight_gradient, head_gradient, pooled_gradient)


def solution(mesh):
    placed = (
        P("dp", None, "mp"),
        P(None, "dp", None, None),
        P(None, "dp", None, None),
        P("dp"),
        P("dp"),
        P(),
        P(None, "dp"),
        P("mp", "dp"),
        P("dp"),
        P("dp"),
    )
    return jax.shard_map(
        shards,
        mesh=mesh,
        in_specs=placed,
        out_specs=(P("dp", None, "mp"), P(), P(), P("mp", "dp"), P("dp"), P("dp", "mp")),
        check_vma=False,
    )
```

```python
import functools
import math

import jax
import jax.numpy as jnp
from jax import lax
from jax.experimental import pallas as pl
from jax.experimental.pallas import tpu as pltpu
from jax.sharding import PartitionSpec as P

D = 8192
HD = 128
Q_HEADS = 48
KV_HEADS = 6


EPSILON = 1e-05


def bradley_terry(rewards, pairing):
    count = rewards.shape[0]
    chosen = pairing[0::2, None] == jnp.arange(count)[None, :]
    rejected = pairing[1::2, None] == jnp.arange(count)[None, :]
    sign = chosen.astype(jnp.float32) - rejected.astype(jnp.float32)
    margin = jnp.sum(sign * rewards[None, :], axis=1)
    loss_value = jnp.mean(jax.nn.softplus(-margin))
    slope = -jax.nn.sigmoid(-margin) / margin.shape[0]
    reward_slope = jnp.sum(sign * slope[:, None], axis=0)
    return (loss_value, reward_slope)


def pack_kernel(window, meta, query, keys, out, late):
    slots = out.shape[0]
    rest = late.shape[2]
    width = query.shape[2] - rest
    span = window * HD
    first = pl.multiple_of(meta[2 * slots] * HD, HD)

    def body(p, carry):
        r = meta[p]
        out[p, :, pl.ds(0, width)] = query[r, :, pl.ds(0, width)]
        late[p] = query[r, :, pl.ds(width, rest)]
        out[p, :, pl.ds(width, span)] = keys[0, r, :, pl.ds(first, span)]
        out[p, :, pl.ds(width + span, span)] = keys[1, r, :, pl.ds(first, span)]
        length = meta[slots + p].astype(jnp.float32)
        place = r.astype(jnp.float32)
        lane = lax.broadcasted_iota(jnp.int32, (out.shape[1], HD), 1)
        out[p, :, pl.ds(width + 2 * span, HD)] = jnp.where(lane < HD // 2, length, place).astype(
            jnp.bfloat16
        )
        return carry

    lax.fori_loop(0, slots, body, 0)


def attention_kernel(slot_count, placed, meta, query, own_k, own_v, lens, cache, out, pooled):
    rows = query.shape[0]
    head = pl.program_id(0)
    chunk = 128
    blocks = chunk // slot_count
    scale = math.log2(math.e) / math.sqrt(HD)
    contract = (((1,), (1,)), ((), ()))
    row = lax.broadcasted_iota(jnp.int32, (chunk, chunk), 0)
    col = lax.broadcasted_iota(jnp.int32, (chunk, chunk), 1)
    t = row % slot_count
    s = col % slot_count
    causal = (row // slot_count == col // slot_count) & (s <= t)
    s_float = s.astype(jnp.float32)
    t_float = t.astype(jnp.float32)
    gather = lax.broadcasted_iota(jnp.int32, (blocks, chunk), 0)
    member = lax.broadcasted_iota(jnp.int32, (blocks, chunk), 1)
    gather = jnp.where(gather == member // slot_count, 1.0, 0.0).astype(jnp.bfloat16)
    for start in range(0, rows, chunk):
        here = pl.ds(start, chunk)
        q = query[here, :]
        length = jnp.broadcast_to(lens[here, :].astype(jnp.float32)[:, 0:1], (chunk, chunk))
        far = lax.dot_general(q, cache[0, 0], contract, preferred_element_type=jnp.float32)
        near = lax.dot_general(q, own_k[here, :], contract, preferred_element_type=jnp.float32)
        near = jnp.where(causal & (s_float < length), near, -jnp.inf)
        top = jnp.maximum(
            jnp.max(far, axis=1, keepdims=True), jnp.max(near, axis=1, keepdims=True)
        )
        far = jnp.exp2((far - top) * scale)
        near = jnp.exp2((near - top) * scale)
        total = jnp.sum(far, axis=1, keepdims=True) + jnp.sum(near, axis=1, keepdims=True)
        value = jnp.dot(far.astype(jnp.bfloat16), cache[1, 0], preferred_element_type=jnp.float32)
        value += jnp.dot(
            near.astype(jnp.bfloat16), own_v[here, :], preferred_element_type=jnp.float32
        )
        value = jnp.where(t_float < length, value / total, 0.0)
        out[here, :] = value.astype(jnp.bfloat16)
        last = jnp.where(t_float == length - 1.0, value, 0.0)
        last = jnp.dot(gather, last.astype(jnp.bfloat16), preferred_element_type=jnp.float32)
        there = pl.ds(start // slot_count, blocks)
        pooled[there, pl.ds(pl.multiple_of(head * HD, HD), HD)] = last.astype(jnp.bfloat16)

        if placed:

            @pl.when(head == 0)
            def _():
                place = lens[here, :].astype(jnp.float32).reshape(blocks, slot_count, HD)
                pooled[there, pl.ds(pooled.shape[1] - HD, HD)] = jnp.max(place, axis=1).astype(
                    jnp.bfloat16
                )


def unpack_kernel(meta, returned, out):
    def body(r, carry):
        out[r] = returned[meta[r]]
        return carry

    lax.fori_loop(0, out.shape[0], body, 0)


def shards(
    response_query,
    response_keys,
    prompt_cache,
    lengths,
    owners,
    pairing,
    residual,
    output_weight,
    norm_gain,
    reward_head,
):
    groups = lax.axis_size("dp")
    planes = lax.axis_size("mp")
    model_rank = lax.axis_index("mp")
    held_count, slot_count, head_width = response_query.shape
    local_heads = head_width // HD
    group_size = Q_HEADS // KV_HEADS
    per_owner = (held_count + groups - 1) // groups
    capacity = groups * per_owner
    window = max(
        (m * local_heads + local_heads - 1) // group_size - m * local_heads // group_size + 1
        for m in range(planes)
    )
    first_head = jnp.minimum(model_rank * local_heads // group_size, KV_HEADS - window)
    head_kv = (model_rank * local_heads + jnp.arange(local_heads)) // group_size
    positions = jnp.arange(held_count)
    earlier = (owners[None, :] == owners[:, None]) & (positions[None, :] < positions[:, None])
    target = (owners * per_owner + jnp.sum(earlier, axis=1)).astype(jnp.int32)
    sent_from = (target[None, :] == jnp.arange(capacity)[:, None]).astype(jnp.int32)
    source = jnp.sum(sent_from * positions[None, :], axis=1)
    slot_length = jnp.sum(sent_from * lengths[None, :], axis=1)
    params = pltpu.CompilerParams(vmem_limit_bytes=40 * 1024 * 1024)
    vmem = pl.BlockSpec(memory_space=pltpu.VMEM)
    smem = pl.BlockSpec(memory_space=pltpu.SMEM)
    early = local_heads - local_heads // 2
    late_width = local_heads // 2 * HD
    packed_width = early * HD + (2 * window + 1) * HD
    packed, late = pl.pallas_call(
        functools.partial(pack_kernel, window),
        out_shape=(
            jax.ShapeDtypeStruct((capacity, slot_count, packed_width), jnp.bfloat16),
            jax.ShapeDtypeStruct((capacity, slot_count, late_width), jnp.bfloat16),
        ),
        in_specs=[smem, vmem, vmem],
        out_specs=(vmem, vmem),
        compiler_params=params,
        name="pack",
    )(
        jnp.concatenate([source, slot_length, first_head[None]]).astype(jnp.int32),
        response_query,
        response_keys,
    )
    packed = packed.reshape(groups, per_owner, slot_count, packed_width)
    arrived = lax.all_to_all(packed, "dp", split_axis=0, concat_axis=0, tiled=True)
    late = late.reshape(groups, per_owner, slot_count, late_width)
    late = lax.all_to_all(late, "dp", split_axis=0, concat_axis=0, tiled=True)
    rows = capacity * slot_count
    late = late.reshape(rows, late_width)
    arrived = arrived.reshape(rows, packed_width)
    block = (rows, HD)

    def attend(query, head_base, heads, placed):
        pooled_width = (heads + placed) * HD
        at = lambda meta, h: meta[local_heads + head_base + h]
        return pl.pallas_call(
            functools.partial(attention_kernel, slot_count, placed),
            out_shape=(
                jax.ShapeDtypeStruct((rows, heads * HD), jnp.bfloat16),
                jax.ShapeDtypeStruct((capacity, pooled_width), jnp.bfloat16),
            ),
            grid_spec=pltpu.PrefetchScalarGridSpec(
                num_scalar_prefetch=1,
                grid=(heads,),
                in_specs=[
                    pl.BlockSpec(block, lambda h, meta: (0, h)),
                    pl.BlockSpec(block, lambda h, meta: (0, early + at(meta, h))),
                    pl.BlockSpec(block, lambda h, meta: (0, early + window + at(meta, h))),
                    pl.BlockSpec(block, lambda h, meta: (0, early + 2 * window)),
                    pl.BlockSpec(
                        (2, 1, prompt_cache.shape[2], HD),
                        lambda h, meta: (0, 0, 0, meta[head_base + h]),
                    ),
                ],
                out_specs=(
                    pl.BlockSpec(block, lambda h, meta: (0, h)),
                    pl.BlockSpec((capacity, pooled_width), lambda h, meta: (0, 0)),
                ),
            ),
            compiler_params=params,
            cost_estimate=pl.CostEstimate(
                flops=4 * rows * heads * HD * prompt_cache.shape[2],
                bytes_accessed=8 * rows * heads * HD,
                transcendentals=rows * heads * prompt_cache.shape[2],
            ),
            name="attention_early" if placed else "attention_late",
        )(
            jnp.concatenate([head_kv, head_kv - first_head]).astype(jnp.int32),
            query,
            arrived,
            arrived,
            arrived,
            prompt_cache,
        )

    def share_rows(own):
        copies = jnp.broadcast_to(own[None], (groups,) + own.shape)
        copies = lax.all_to_all(copies, "dp", split_axis=0, concat_axis=0, tiled=True)
        return copies.reshape(groups * own.shape[0], own.shape[1])

    attended_early, pooled_early = attend(arrived, 0, early, True)
    pooled_slots = share_rows(pooled_early)
    attended_late, pooled_late = attend(late, early, local_heads - early, False)
    pooled_late = share_rows(pooled_late)
    attended = jnp.concatenate([attended_early, attended_late], axis=1)
    result = attended.reshape(groups, per_owner, slot_count, head_width)
    returned = lax.all_to_all(result, "dp", split_axis=0, concat_axis=0, tiled=True)
    attention_rows = pl.pallas_call(
        unpack_kernel,
        out_shape=jax.ShapeDtypeStruct(response_query.shape, jnp.bfloat16),
        in_specs=[smem, vmem],
        out_specs=vmem,
        compiler_params=params,
        name="unpack",
    )(target, returned.reshape(capacity, slot_count, head_width))
    count = held_count * groups
    sender = jnp.arange(capacity * groups) % capacity // per_owner
    place = pooled_slots[:, early * HD + HD - 1].astype(jnp.int32)
    live = pooled_slots[:, early * HD] > 0
    response = jnp.where(live, sender * held_count + place, count)
    order = (jnp.arange(count)[:, None] == response[None, :]).astype(jnp.bfloat16)
    pooled_all = jnp.concatenate(
        [
            jnp.dot(order, slots, preferred_element_type=jnp.float32).astype(jnp.bfloat16)
            for slots in (pooled_slots[:, : early * HD], pooled_late)
        ],
        axis=1,
    )
    share = count // planes
    partial_mix = jnp.dot(pooled_all, output_weight, preferred_element_type=jnp.float32)
    columns = output_weight.shape[1]
    scaled_head = norm_gain * reward_head
    shares = lax.all_to_all(
        partial_mix.astype(jnp.bfloat16).reshape(planes, share, columns),
        "mp",
        split_axis=0,
        concat_axis=0,
        tiled=True,
    )
    part = jnp.sum(shares.astype(jnp.float32), axis=0) + lax.dynamic_slice_in_dim(
        residual, model_rank * share, share, 0
    ).astype(jnp.float32)
    combined = lax.all_gather(part.astype(jnp.bfloat16), "mp", axis=0, tiled=True).astype(
        jnp.float32
    )
    square_sum = jnp.sum(combined * combined, axis=1)
    signal = jnp.sum(combined * scaled_head[None, :], axis=1)
    square_sum, signal = lax.psum((square_sum, signal), "dp")
    inverse = lax.rsqrt(square_sum / D + EPSILON)
    rewards = inverse * signal
    pair_loss, reward_slope = bradley_terry(rewards, pairing)
    direct_term = reward_slope * inverse
    norm_term = reward_slope * inverse * inverse * inverse * signal / D
    upstream = direct_term[:, None] * scaled_head[None, :] - norm_term[:, None] * combined
    head_gradient = jnp.sum(direct_term[:, None] * combined * norm_gain[None, :], axis=0)
    upstream_half = upstream.astype(jnp.bfloat16)
    slope_part = lax.dot_general(
        upstream_half,
        output_weight,
        (((1,), (1,)), ((), ())),
        preferred_element_type=jnp.float32,
    ).astype(jnp.bfloat16)
    slope_parts = lax.all_to_all(
        slope_part.reshape(groups, held_count, head_width),
        "dp",
        split_axis=0,
        concat_axis=0,
        tiled=True,
    )
    weight_gradient = lax.dot_general(
        pooled_all, upstream_half, (((0,), (0,)), ((), ())), preferred_element_type=jnp.float32
    )
    pooled_gradient = jnp.sum(slope_parts.astype(jnp.float32), axis=0)
    return (attention_rows, rewards, pair_loss, weight_gradient, head_gradient, pooled_gradient)


def solution(mesh):
    placed = (
        P("dp", None, "mp"),
        P(None, "dp", None, None),
        P(None, "dp", None, None),
        P("dp"),
        P("dp"),
        P(),
        P(None, "dp"),
        P("mp", "dp"),
        P("dp"),
        P("dp"),
    )
    return jax.shard_map(
        shards,
        mesh=mesh,
        in_specs=placed,
        out_specs=(P("dp", None, "mp"), P(), P(), P("mp", "dp"), P("dp"), P("dp", "mp")),
        check_vma=False,
    )
```

```python
import functools
import math

import jax
import jax.numpy as jnp
from jax import lax
from jax.experimental import pallas as pl
from jax.experimental.pallas import tpu as pltpu
from jax.sharding import PartitionSpec as P

D = 8192
HD = 128
Q_HEADS = 48
KV_HEADS = 6


EPSILON = 1e-05


def bradley_terry(rewards, pairing):
    count = rewards.shape[0]
    chosen = pairing[0::2, None] == jnp.arange(count)[None, :]
    rejected = pairing[1::2, None] == jnp.arange(count)[None, :]
    sign = chosen.astype(jnp.float32) - rejected.astype(jnp.float32)
    margin = jnp.sum(sign * rewards[None, :], axis=1)
    loss_value = jnp.mean(jax.nn.softplus(-margin))
    slope = -jax.nn.sigmoid(-margin) / margin.shape[0]
    reward_slope = jnp.sum(sign * slope[:, None], axis=0)
    return (loss_value, reward_slope)


def pack_kernel(window, meta, query, keys, out, late):
    slots = out.shape[0]
    rest = late.shape[2]
    width = query.shape[2] - rest
    span = window * HD
    first = pl.multiple_of(meta[2 * slots] * HD, HD)

    def body(p, carry):
        r = meta[p]
        out[p, :, pl.ds(0, width)] = query[r, :, pl.ds(0, width)]
        late[p] = query[r, :, pl.ds(width, rest)]
        out[p, :, pl.ds(width, span)] = keys[0, r, :, pl.ds(first, span)]
        out[p, :, pl.ds(width + span, span)] = keys[1, r, :, pl.ds(first, span)]
        length = meta[slots + p].astype(jnp.float32)
        place = r.astype(jnp.float32)
        lane = lax.broadcasted_iota(jnp.int32, (out.shape[1], HD), 1)
        out[p, :, pl.ds(width + 2 * span, HD)] = jnp.where(lane < HD // 2, length, place).astype(
            jnp.bfloat16
        )
        return carry

    lax.fori_loop(0, slots, body, 0)


def attention_kernel(slot_count, meta, query, own_k, own_v, lens, cache, out):
    rows = query.shape[0]
    chunk = 128
    scale = math.log2(math.e) / math.sqrt(HD)
    contract = (((1,), (1,)), ((), ()))
    row = lax.broadcasted_iota(jnp.int32, (chunk, chunk), 0)
    col = lax.broadcasted_iota(jnp.int32, (chunk, chunk), 1)
    t = row % slot_count
    s = col % slot_count
    causal = (row // slot_count == col // slot_count) & (s <= t)
    s_float = s.astype(jnp.float32)
    t_float = t.astype(jnp.float32)
    for start in range(0, rows, chunk):
        here = pl.ds(start, chunk)
        q = query[here, :]
        length = jnp.broadcast_to(lens[here, :].astype(jnp.float32)[:, 0:1], (chunk, chunk))
        far = lax.dot_general(q, cache[0, 0], contract, preferred_element_type=jnp.float32)
        near = lax.dot_general(q, own_k[here, :], contract, preferred_element_type=jnp.float32)
        near = jnp.where(causal & (s_float < length), near, -jnp.inf)
        top = jnp.maximum(
            jnp.max(far, axis=1, keepdims=True), jnp.max(near, axis=1, keepdims=True)
        )
        far = jnp.exp2((far - top) * scale)
        near = jnp.exp2((near - top) * scale)
        total = jnp.sum(far, axis=1, keepdims=True) + jnp.sum(near, axis=1, keepdims=True)
        value = jnp.dot(far.astype(jnp.bfloat16), cache[1, 0], preferred_element_type=jnp.float32)
        value += jnp.dot(
            near.astype(jnp.bfloat16), own_v[here, :], preferred_element_type=jnp.float32
        )
        value = jnp.where(t_float < length, value / total, 0.0)
        out[here, :] = value.astype(jnp.bfloat16)


def unpack_kernel(meta, returned, out):
    def body(r, carry):
        out[r] = returned[meta[r]]
        return carry

    lax.fori_loop(0, out.shape[0], body, 0)


def shards(
    response_query,
    response_keys,
    prompt_cache,
    lengths,
    owners,
    pairing,
    residual,
    output_weight,
    norm_gain,
    reward_head,
):
    groups = lax.axis_size("dp")
    planes = lax.axis_size("mp")
    model_rank = lax.axis_index("mp")
    held_count, slot_count, head_width = response_query.shape
    local_heads = head_width // HD
    group_size = Q_HEADS // KV_HEADS
    per_owner = (held_count + groups - 1) // groups
    capacity = groups * per_owner
    window = max(
        (m * local_heads + local_heads - 1) // group_size - m * local_heads // group_size + 1
        for m in range(planes)
    )
    first_head = jnp.minimum(model_rank * local_heads // group_size, KV_HEADS - window)
    head_kv = (model_rank * local_heads + jnp.arange(local_heads)) // group_size
    positions = jnp.arange(held_count)
    earlier = (owners[None, :] == owners[:, None]) & (positions[None, :] < positions[:, None])
    target = (owners * per_owner + jnp.sum(earlier, axis=1)).astype(jnp.int32)
    sent_from = (target[None, :] == jnp.arange(capacity)[:, None]).astype(jnp.int32)
    source = jnp.sum(sent_from * positions[None, :], axis=1)
    slot_length = jnp.sum(sent_from * lengths[None, :], axis=1)
    params = pltpu.CompilerParams(vmem_limit_bytes=40 * 1024 * 1024)
    vmem = pl.BlockSpec(memory_space=pltpu.VMEM)
    smem = pl.BlockSpec(memory_space=pltpu.SMEM)
    early = local_heads - local_heads // 2
    late_width = local_heads // 2 * HD
    packed_width = early * HD + (2 * window + 1) * HD
    packed, late = pl.pallas_call(
        functools.partial(pack_kernel, window),
        out_shape=(
            jax.ShapeDtypeStruct((capacity, slot_count, packed_width), jnp.bfloat16),
            jax.ShapeDtypeStruct((capacity, slot_count, late_width), jnp.bfloat16),
        ),
        in_specs=[smem, vmem, vmem],
        out_specs=(vmem, vmem),
        compiler_params=params,
        name="pack",
    )(
        jnp.concatenate([source, slot_length, first_head[None]]).astype(jnp.int32),
        response_query,
        response_keys,
    )
    packed = packed.reshape(groups, per_owner, slot_count, packed_width)
    arrived = lax.all_to_all(packed, "dp", split_axis=0, concat_axis=0, tiled=True)
    late = late.reshape(groups, per_owner, slot_count, late_width)
    late = lax.all_to_all(late, "dp", split_axis=0, concat_axis=0, tiled=True)
    rows = capacity * slot_count
    late = late.reshape(rows, late_width)
    arrived = arrived.reshape(rows, packed_width)
    block = (rows, HD)

    def attend(query, head_base, heads):
        at = lambda meta, h: meta[local_heads + head_base + h]
        return pl.pallas_call(
            functools.partial(attention_kernel, slot_count),
            out_shape=jax.ShapeDtypeStruct((rows, heads * HD), jnp.bfloat16),
            grid_spec=pltpu.PrefetchScalarGridSpec(
                num_scalar_prefetch=1,
                grid=(heads,),
                in_specs=[
                    pl.BlockSpec(block, lambda h, meta: (0, h)),
                    pl.BlockSpec(block, lambda h, meta: (0, early + at(meta, h))),
                    pl.BlockSpec(block, lambda h, meta: (0, early + window + at(meta, h))),
                    pl.BlockSpec(block, lambda h, meta: (0, early + 2 * window)),
                    pl.BlockSpec(
                        (2, 1, prompt_cache.shape[2], HD),
                        lambda h, meta: (0, 0, 0, meta[head_base + h]),
                    ),
                ],
                out_specs=pl.BlockSpec(block, lambda h, meta: (0, h)),
            ),
            compiler_params=params,
            cost_estimate=pl.CostEstimate(
                flops=4 * rows * heads * HD * prompt_cache.shape[2],
                bytes_accessed=8 * rows * heads * HD,
                transcendentals=rows * heads * prompt_cache.shape[2],
            ),
            name="attention_late" if head_base else "attention_early",
        )(
            jnp.concatenate([head_kv, head_kv - first_head]).astype(jnp.int32),
            query,
            arrived,
            arrived,
            arrived,
            prompt_cache,
        )

    def share_rows(own):
        copies = jnp.broadcast_to(own[None], (groups,) + own.shape)
        copies = lax.all_to_all(copies, "dp", split_axis=0, concat_axis=0, tiled=True)
        return copies.reshape(groups * own.shape[0], own.shape[1])

    tags = arrived.reshape(capacity, slot_count, packed_width)[:, 0, packed_width - HD :]
    last_row = tags[:, :1].astype(jnp.int32) - 1 == jnp.arange(slot_count)[None, :]

    def last_rows(attended):
        by_block = attended.reshape(capacity, slot_count, attended.shape[1]).astype(jnp.float32)
        return jnp.sum(jnp.where(last_row[:, :, None], by_block, 0.0), axis=1).astype(jnp.bfloat16)

    attended_early = attend(arrived, 0, early)
    pooled_early = jnp.concatenate([last_rows(attended_early), tags], axis=1)
    pooled_slots = share_rows(pooled_early)
    attended_late = attend(late, early, local_heads - early)
    pooled_late = last_rows(attended_late)
    pooled_late = share_rows(pooled_late)
    attended = jnp.concatenate([attended_early, attended_late], axis=1)
    result = attended.reshape(groups, per_owner, slot_count, head_width)
    returned = lax.all_to_all(result, "dp", split_axis=0, concat_axis=0, tiled=True)
    attention_rows = pl.pallas_call(
        unpack_kernel,
        out_shape=jax.ShapeDtypeStruct(response_query.shape, jnp.bfloat16),
        in_specs=[smem, vmem],
        out_specs=vmem,
        compiler_params=params,
        name="unpack",
    )(target, returned.reshape(capacity, slot_count, head_width))
    count = held_count * groups
    sender = jnp.arange(capacity * groups) % capacity // per_owner
    place = pooled_slots[:, early * HD + HD - 1].astype(jnp.int32)
    live = pooled_slots[:, early * HD] > 0
    response = jnp.where(live, sender * held_count + place, count)
    order = (jnp.arange(count)[:, None] == response[None, :]).astype(jnp.bfloat16)
    pooled_all = jnp.concatenate(
        [
            jnp.dot(order, slots, preferred_element_type=jnp.float32).astype(jnp.bfloat16)
            for slots in (pooled_slots[:, : early * HD], pooled_late)
        ],
        axis=1,
    )
    share = count // planes
    partial_mix = jnp.dot(pooled_all, output_weight, preferred_element_type=jnp.float32)
    columns = output_weight.shape[1]
    scaled_head = norm_gain * reward_head
    shares = lax.all_to_all(
        partial_mix.astype(jnp.bfloat16).reshape(planes, share, columns),
        "mp",
        split_axis=0,
        concat_axis=0,
        tiled=True,
    )
    part = jnp.sum(shares.astype(jnp.float32), axis=0) + lax.dynamic_slice_in_dim(
        residual, model_rank * share, share, 0
    ).astype(jnp.float32)
    combined = lax.all_gather(part.astype(jnp.bfloat16), "mp", axis=0, tiled=True).astype(
        jnp.float32
    )
    square_sum = jnp.sum(combined * combined, axis=1)
    signal = jnp.sum(combined * scaled_head[None, :], axis=1)
    square_sum, signal = lax.psum((square_sum, signal), "dp")
    inverse = lax.rsqrt(square_sum / D + EPSILON)
    rewards = inverse * signal
    pair_loss, reward_slope = bradley_terry(rewards, pairing)
    direct_term = reward_slope * inverse
    norm_term = reward_slope * inverse * inverse * inverse * signal / D
    upstream = direct_term[:, None] * scaled_head[None, :] - norm_term[:, None] * combined
    head_gradient = jnp.sum(direct_term[:, None] * combined * norm_gain[None, :], axis=0)
    upstream_half = upstream.astype(jnp.bfloat16)
    slope_part = lax.dot_general(
        upstream_half,
        output_weight,
        (((1,), (1,)), ((), ())),
        preferred_element_type=jnp.float32,
    ).astype(jnp.bfloat16)
    slope_parts = lax.all_to_all(
        slope_part.reshape(groups, held_count, head_width),
        "dp",
        split_axis=0,
        concat_axis=0,
        tiled=True,
    )
    weight_gradient = lax.dot_general(
        pooled_all, upstream_half, (((0,), (0,)), ((), ())), preferred_element_type=jnp.float32
    )
    pooled_gradient = jnp.sum(slope_parts.astype(jnp.float32), axis=0)
    return (attention_rows, rewards, pair_loss, weight_gradient, head_gradient, pooled_gradient)


def solution(mesh):
    placed = (
        P("dp", None, "mp"),
        P(None, "dp", None, None),
        P(None, "dp", None, None),
        P("dp"),
        P("dp"),
        P(),
        P(None, "dp"),
        P("mp", "dp"),
        P("dp"),
        P("dp"),
    )
    return jax.shard_map(
        shards,
        mesh=mesh,
        in_specs=placed,
        out_specs=(P("dp", None, "mp"), P(), P(), P("mp", "dp"), P("dp"), P("dp", "mp")),
        check_vma=False,
    )
```
